32 devices in a mesh: axial: 8 (over y, x, core), pitch: 4 (over z).
Axes of the slice: x: 2, y: 2, z: 4, core: 2. Of those that a mesh axis runs over, the one named last changes fastest.
Arguments:
- fluid_temp: float32 [512, 256, 128], P('axial', 'pitch'), may hold values from -6 to 6
- axial_speed: float32 [512, 256, 128], P('axial', 'pitch'), may hold values from 0.05 to 0.4
- pitch_speed: float32 [512, 256, 128], P('axial', 'pitch'), may hold values from -0.25 to 0.25
- fourier_store: float32 [2, 512, 128], P(None, 'axial'), may hold values from -6 to 6
- wall_temp: float32 [32768, 128], P(('axial', 'pitch')), may hold values from -6 to 6
- wall_cell: int32 [32768], P(('axial', 'pitch')), may hold values from 0 to 4095
- wall_owner: int32 [32768, 1], P(('axial', 'pitch')), may hold values from 0 to 31; in each aligned block of 1024 rows (0 to 1023, 1024 to 2047, ...) at most 64 rows name the same one
- wall_target: int32 [32768], P(('axial', 'pitch')), may hold values from 0 to 127
- wall_count: int32 [32], P(('axial', 'pitch')), may hold values from 1 to 1024, 24576 in all
- metal_temp: float32 [512, 48, 512], P('axial', None, 'pitch'), may hold values from -6 to 6
- metal_diag: float32 [512, 48, 512], P('axial', None, 'pitch'), may hold values from 0.5 to 2
Outputs:
- fluid_out: float32 [512, 256, 128], P('axial', 'pitch')
- metal_out: float32 [512, 48, 512], P('axial', None, 'pitch')
- wall_update: float32 [32768, 128], P(('axial', 'pitch'))
The draws below stay inside these ranges and needn't reach their ends.
Inputs may be any that keep to these rules, and one draw needn't show every extreme that they name: `wall_owner`: within the rows of one device no owner appears more than 64 times, and some owner appears exactly 64 times. `wall_count`: some device has all 1024 rows live.
All inputs are finite; a program needn't handle non-finite values.
Results may differ from the reference program's by a relative error of at most 0.0003.
Values sent between devices are 32-bit elements; how exact they have to be, the bound alone decides.
A program may use at most 192 MiB of HBM per device.

```python
import math
import jax
import jax.numpy as jnp
import numpy as np

CA = 64
CP = 64
NR = 128
MC = 64
MT = 48
SWEEPS = 4
WALL_DEV = 1024
CAP = 64
NA = 512
NP = 256
NCH = 512
NSP = 512
WALL_ROWS = 32768
N_PITCH = 4
DEVICES = 32


def place_ends(values, key, low, largest):
    index_at = [jax.random.randint(jax.random.fold_in(key, axis), (), 0, length) for axis, length in enumerate(values.shape)]
    main_axis = values.shape.index(max(values.shape))
    neighbour = index_at[:main_axis] + [(index_at[main_axis] + 1) % values.shape[main_axis]] + index_at[main_axis + 1:]
    return values.at[tuple(index_at)].set(low).at[tuple(neighbour)].set(largest)


def levels(stream_key, extent, cuts, low, high):
    factor_of, own = 1.0, jax.random.fold_in(stream_key, 6)
    for position, shards_of in cuts:
        heights = jnp.exp(jax.random.uniform(jax.random.fold_in(own, position), (shards_of,), jnp.float32, low / len(cuts), high / len(cuts)))
        factor_of = factor_of * jnp.repeat(heights, extent[position] // shards_of).reshape([-1 if axis == position else 1 for axis in range(len(extent))])
    return factor_of


def split_up(count, total, reach, lean):
    weights = [(1 << 20) // math.isqrt(standing ** lean) + 1 for standing in range(2, count + 1)]
    surplus, counts = total - reach - (count - 1), [1] * (count - 1)
    while surplus > 0:
        movable = [i for i in range(count - 1) if counts[i] < reach]
        mass, remaining = sum([weights[i] for i in movable]), surplus
        for i in movable:
            addition = min(reach - counts[i], max(1, remaining * weights[i] // mass), surplus)
            counts[i] = counts[i] + addition
            surplus = surplus - addition
    return np.array([reach] + counts)


def uneven(key, number_of, total, most, skew):
    if number_of == 2:
        one = jax.random.randint(key, (), max(1, total - most), min(most, total - 1) + 1)
        return jnp.stack([one, total - one])
    lengths = jnp.asarray(split_up(number_of, total, most, skew), jnp.int32)
    couples = (number_of - 1) // 2
    source_of, receiver = lengths[1:1 + 2 * couples:2], lengths[2:2 + 2 * couples:2]
    room = jnp.minimum(source_of - 1, most - receiver)
    passed = jax.random.randint(jax.random.fold_in(key, 1), (couples,), 0, 1 << 20) % (room + 1)
    lengths = lengths.at[1:1 + 2 * couples:2].set(source_of - passed).at[2:2 + 2 * couples:2].set(receiver + passed)
    return lengths[jax.random.permutation(jax.random.fold_in(key, 2), number_of)]


def shared_out(stream_key, own, number, rows, number_of, top, most, lean):
    sequence = jax.random.permutation(stream_key, number_of)
    packed, common = load_shares(number_of, rows * top, most, lean, True), load_shares(number_of, rows * top, most, lean, False)
    places = jnp.arange(number_of)

    def named(lengths, offset_by):
        used = int((lengths > 0).sum())
        fixed = max(1, used // 4)
        passed = fixed + (places - fixed + offset_by * (used - fixed)) % max(1, number_of - fixed)
        return jnp.zeros((number_of,), jnp.int32).at[sequence[jnp.where(places < fixed, places, passed)]].set(jnp.asarray(lengths, jnp.int32))

    lengths = jnp.where(number % 4 == 0, named(packed, number // 4), named(common, number - number // 4 - 1))
    mixed = jax.random.permutation(jax.random.fold_in(own, 3), number_of)
    giver, taker = mixed[0:number_of // 2 * 2:2], mixed[1:number_of // 2 * 2:2]
    margin = jnp.minimum(lengths[giver] - 1, most - lengths[taker]) // 2
    margin = jnp.where((giver == sequence[0]) | (taker == sequence[0]) | (lengths[taker] == 0), 0, jnp.maximum(margin, 0))
    passed = jax.random.randint(jax.random.fold_in(own, 4), (number_of // 2,), 0, 1 << 20) % (margin + 1)
    lengths = lengths.at[giver].add(-passed).at[taker].add(passed)
    items = jnp.searchsorted(jnp.cumsum(lengths), jnp.arange(rows * top), side="right").astype(jnp.int32)
    grid = items.reshape(top, rows).T
    grid = grid[jax.random.permutation(jax.random.fold_in(own, 1), rows)]
    offset_by = jax.random.randint(jax.random.fold_in(own, 2), (rows, 1), 0, top)
    return jnp.take_along_axis(grid, (jnp.arange(top)[None, :] + offset_by) % top, axis=1)


def load_shares(count, total, reach, skew, full):
    weights = [(1 << 20) // math.isqrt(rank ** skew) + 1 for rank in range(1, count + 1)]
    largest = reach if full else min(reach, max(-(-total // count), total * weights[0] // sum(weights)))
    least = 1 if total - largest >= count - 1 else 0
    holding, spare = [largest] + [least] * (count - 1), total - largest - least * (count - 1)
    while spare > 0:
        movable = [i for i in range(1, count) if holding[i] < largest] or [i for i in range(1, count) if holding[i] < reach]
        mass, budget = sum([weights[i] for i in movable]), spare
        for i in movable:
            more = min(reach - holding[i], max(1, budget * weights[i] // mass), spare)
            holding[i] = holding[i] + more
            spare = spare - more
    return np.array(holding)


def normal_values(own_key, extent, deviation, reach, split=(), held_as=jnp.bfloat16):
    gain = levels(own_key, extent, split, -0.22, 0.18) if split else 1.0
    drawn = jax.random.normal(own_key, extent, jnp.float32) * deviation * gain
    return jnp.minimum(jnp.maximum(drawn, -reach), reach).astype(held_as)


def setup_inputs(seed: int = 0) -> dict:
    splits = jax.random.split(jax.random.key(seed), 12)
    fluid_temp = normal_values(splits[0], (NA, NP, NR), 1.0, 6.0, ((0, 8), (1, 4)), jnp.float32)
    axial_speed = jnp.clip(0.05 + 0.35 * jax.random.uniform(splits[1], (NA, NP, NR), jnp.float32) ** levels(splits[1], (NA, NP, NR), ((0, 8), (1, 4)), -0.2, 0.2), 0.05, 0.4)
    pitch_speed = jnp.clip(jax.random.uniform(splits[2], (NA, NP, NR), jnp.float32, -0.25, 0.25) * levels(splits[2], (NA, NP, NR), ((0, 8), (1, 4)), -0.4, 0.0), -0.25, 0.25)
    fourier_store = normal_values(splits[3], (2, NA, NR), 1.0, 6.0, ((1, 8),), jnp.float32)
    wall_temp = normal_values(splits[4], (WALL_ROWS, NR), 1.0, 6.0, ((0, 32),), jnp.float32)
    wall_cell = place_ends(jax.random.randint(splits[5], (WALL_ROWS,), 0, CA * CP), jax.random.fold_in(splits[5], 1), 0, (CA * CP) - 1).astype(jnp.int32)
    wall_owner_keys = jax.random.split(jax.random.fold_in(splits[6], 1), WALL_ROWS // WALL_DEV)
    wall_owner_turns = jax.random.permutation(jax.random.fold_in(splits[6], 3), WALL_ROWS // WALL_DEV)
    wall_owner = jax.vmap(lambda own, number: shared_out(jax.random.fold_in(splits[6], 2), own, number, WALL_DEV, DEVICES, 1, CAP, 2))(wall_owner_keys, wall_owner_turns).reshape((WALL_ROWS, 1))
    wall_target = place_ends(jax.random.randint(splits[7], (WALL_ROWS,), 0, 2 * MC), jax.random.fold_in(splits[7], 1), 0, (2 * MC) - 1).astype(jnp.int32)
    wall_count = uneven(splits[8], DEVICES, DEVICES * WALL_DEV * 3 // 4, WALL_DEV, 2).astype(jnp.int32)
    metal_temp = normal_values(splits[9], (NCH, MT, NSP), 1.0, 6.0, ((0, 8), (2, 4)), jnp.float32)
    metal_diag = jnp.clip(0.5 + 1.5 * jax.random.uniform(splits[10], (NCH, MT, NSP), jnp.float32) ** levels(splits[10], (NCH, MT, NSP), ((0, 8), (2, 4)), -0.2, 0.2), 0.5, 2.0)
    return {"fluid_temp": fluid_temp, "axial_speed": axial_speed, "pitch_speed": pitch_speed, "fourier_store": fourier_store, "wall_temp": wall_temp, "wall_cell": wall_cell, "wall_owner": wall_owner, "wall_target": wall_target, "wall_count": wall_count, "metal_temp": metal_temp, "metal_diag": metal_diag}


KAPPA = 0.1
HEAT = 0.3
PHASE_COS = 0.8
PHASE_SIN = 0.6
LOW_BOUND = 0.5
HIGH_BOUND = 14.0


def fluid_rate(temp, axial_speed, pitch_speed, fourier_store, sink):
    east = jnp.concatenate([temp[1:], temp[-1:]], 0)
    west = jnp.concatenate([temp[:1], temp[:-1]], 0)
    lower = PHASE_COS * temp[:, -1:] + PHASE_SIN * fourier_store[0][:, None, :]
    upper = PHASE_COS * temp[:, :1] + PHASE_SIN * fourier_store[1][:, None, :]
    north = jnp.concatenate([temp[:, 1:], upper], 1)
    south = jnp.concatenate([lower, temp[:, :-1]], 1)
    outer = jnp.concatenate([temp[:, :, 1:], temp[:, :, -1:]], 2)
    inner = jnp.concatenate([temp[:, :, :1], temp[:, :, :-1]], 2)
    spread = east + west + north + south + outer + inner - 6.0 * temp
    return -0.5 * axial_speed * (east - west) - 0.5 * pitch_speed * (north - south) + KAPPA * spread - sink


def operate(field, diag):
    padded = jnp.pad(field, 1)
    beside = padded[2:, 1:-1, 1:-1] + padded[:-2, 1:-1, 1:-1]
    beside = beside + padded[1:-1, 2:, 1:-1] + padded[1:-1, :-2, 1:-1]
    beside = beside + padded[1:-1, 1:-1, 2:] + padded[1:-1, 1:-1, :-2]
    return (6.0 + diag) * field - beside


def reference(fluid_temp, axial_speed, pitch_speed, fourier_store, wall_temp, wall_cell, wall_owner, wall_target, wall_count, metal_temp, metal_diag):
    rows = jnp.arange(WALL_ROWS, dtype=jnp.int32)
    device = rows // WALL_DEV
    live = (rows % WALL_DEV) < wall_count[device]
    livef = live.astype(jnp.float32)[:, None]
    cell_a = (device // N_PITCH) * CA + wall_cell // CP
    cell_p = (device % N_PITCH) * CP + wall_cell % CP
    flat = (cell_a * NP + cell_p).astype(jnp.int32)

    def wall_flux(temp):
        rows_temp = temp.reshape(NA * NP, NR)[flat]
        return HEAT * (rows_temp - wall_temp) * livef

    def sink_of(flux):
        return jnp.zeros((NA * NP, NR), jnp.float32).at[flat].add(flux).reshape(NA, NP, NR)

    flux_first = wall_flux(fluid_temp)
    section = fluid_temp + fluid_rate(fluid_temp, axial_speed, pitch_speed, fourier_store, sink_of(flux_first))
    flux_second = wall_flux(section)
    fluid_out = 0.5 * (fluid_temp + section + fluid_rate(section, axial_speed, pitch_speed, fourier_store, sink_of(flux_second)))
    flux = 0.5 * (flux_first + flux_second)

    owner = wall_owner[:, 0]
    chord = (owner // N_PITCH) * MC + wall_target // 2
    side = wall_target % 2
    metal_row = ((chord * 2 + side) * N_PITCH + owner % N_PITCH).astype(jnp.int32)
    inject = jnp.zeros((NCH * 2 * N_PITCH, NR), jnp.float32).at[metal_row].add(flux)
    inject = inject.reshape(NCH, 2, NSP)
    rhs = metal_diag * metal_temp
    rhs = rhs.at[:, 0, :].add(inject[:, 0])
    rhs = rhs.at[:, MT - 1, :].add(inject[:, 1])

    theta = 0.5 * (HIGH_BOUND + LOW_BOUND)
    delta = 0.5 * (HIGH_BOUND - LOW_BOUND)
    ratio = theta / delta
    rho = 1.0 / ratio
    solution = metal_temp
    resid = rhs - operate(solution, metal_diag)
    direction = resid / theta
    for sweep in range(SWEEPS):
        solution = solution + direction
        if sweep < SWEEPS - 1:
            resid = resid - operate(direction, metal_diag)
            rho_new = 1.0 / (2.0 * ratio - rho)
            direction = (rho_new * rho) * direction + (2.0 * rho_new / delta) * resid
            rho = rho_new
    metal_out = solution

    bound = jnp.stack([metal_out[:, 0, :], metal_out[:, MT - 1, :]], 1).reshape(NCH * 2 * N_PITCH, NR)
    values = bound[metal_row]
    wall_update = jnp.where(live[:, None], 0.5 * (wall_temp + values), wall_temp)
    return fluid_out, metal_out, wall_update
```

```python
import functools

import jax
import jax.numpy as jnp
from jax import lax
from jax.experimental import pallas as pl
from jax.experimental.pallas import tpu as pltpu
from jax.sharding import PartitionSpec as P

SWEEPS = 4
KAPPA = 0.1
HEAT = 0.3
PHASE_COS = 0.8
PHASE_SIN = 0.6
LOW_BOUND = 0.5
HIGH_BOUND = 14.0
THETA = 0.5 * (HIGH_BOUND + LOW_BOUND)
DELTA = 0.5 * (HIGH_BOUND - LOW_BOUND)
MESH = pl.DeviceIdType.MESH
F32 = jnp.float32
BF16 = jnp.bfloat16


def cheb_factors():
    ratio = THETA / DELTA
    rho = 1.0 / ratio
    factors = []
    for _ in range(SWEEPS - 1):
        rho_new = 1.0 / (2.0 * ratio - rho)
        factors.append((rho_new * rho, 2.0 * rho_new / DELTA))
        rho = rho_new
    return factors


def two_parts(value):
    hi = value.astype(BF16)
    lo = (value - hi.astype(F32)).astype(BF16)
    return hi, lo


def kernel(
    na, npi, cap,
    cell_s, key_s, count_s,
    cell_v, key_v, ids_v, wall, fourier, aspeed, pspeed, diag, fluid_hbm, metal_hbm,
    fluid_out, metal_out, wall_out,
    upad, spad, avg, wsum, wcnt, face, ph, wcat, rows, fcat,
    xpad, da, db, res, mh, mpack, inj,
    snd, rcv, bsnd, brcv,
    lsem, fsend, frecv, msend, mrecv, asend, arecv,
):
    ax = lax.axis_index("axial")
    pz = lax.axis_index("pitch")
    devices = na * npi
    me = ax * npi + pz
    ca, cp, nr = aspeed.shape
    mc, mt, _ = diag.shape
    slots = wall.shape[0]
    group = nr // cap

    def dev(e):
        return (lax.div(e, npi), lax.rem(e, npi))

    up_axial = (jnp.minimum(ax + 1, na - 1), pz)
    dn_axial = (jnp.maximum(ax - 1, 0), pz)
    north_dev = (ax, lax.rem(pz + 1, npi))
    south_dev = (ax, lax.rem(pz + npi - 1, npi))
    has_dn, has_up = ax > 0, ax < na - 1
    has_lo, has_hi = pz > 0, pz < npi - 1

    ucopy = pltpu.make_async_copy(fluid_hbm, upad.at[pl.ds(1, ca)], lsem.at[0])
    xcopy = pltpu.make_async_copy(metal_hbm, xpad.at[pl.ds(1, mc)], lsem.at[1])
    ucopy.start()
    xcopy.start()

    barrier = pltpu.get_barrier_semaphore()

    @pl.loop(1, devices)
    def _(o):
        pl.semaphore_signal(
            barrier, inc=1, device_id=dev(lax.rem(me + o, devices)), device_id_type=MESH
        )

    def remote(src, dst, ssem, rsem, device):
        return pltpu.make_async_remote_copy(
            src_ref=src, dst_ref=dst, send_sem=ssem, recv_sem=rsem,
            device_id=device, device_id_type=MESH,
        )

    def fluid_copies(pad, st):
        return (
            (has_up, has_dn, remote(pad.at[ca], pad.at[0], fsend.at[st, 0], frecv.at[st, 0], up_axial)),
            (has_dn, has_up, remote(pad.at[1], pad.at[ca + 1], fsend.at[st, 1], frecv.at[st, 1], dn_axial)),
            (None, None, remote(face.at[st, 1], ph.at[st, 0], fsend.at[st, 2], frecv.at[st, 2], north_dev)),
            (None, None, remote(face.at[st, 0], ph.at[st, 1], fsend.at[st, 3], frecv.at[st, 3], south_dev)),
        )

    def metal_copies(pad, st):
        return (
            (has_up, has_dn, remote(pad.at[mc], mh.at[st, 0], msend.at[st, 0], mrecv.at[st, 0], up_axial)),
            (has_dn, has_up, remote(pad.at[1], mh.at[st, 1], msend.at[st, 1], mrecv.at[st, 1], dn_axial)),
            (has_hi, has_lo, remote(mpack.at[st], mh.at[st, 2], msend.at[st, 2], mrecv.at[st, 2], north_dev)),
            (has_lo, has_hi, remote(mpack.at[st], mh.at[st, 3], msend.at[st, 3], mrecv.at[st, 3], south_dev)),
        )

    def when(condition, action):
        if condition is None:
            action()
        else:
            pl.when(condition)(action)

    def start(copies):
        for sends, _, copy in copies:
            when(sends, copy.start)

    def wait_sent(copies):
        for sends, _, copy in copies:
            when(sends, copy.wait_send)

    def wait_got(copies):
        for _, gets, copy in copies:
            when(gets, copy.wait_recv)

    lane_m = lax.broadcasted_iota(jnp.int32, (mt, nr), 1)
    row_m = lax.broadcasted_iota(jnp.int32, (mt, nr), 0)
    lane_f = lax.broadcasted_iota(jnp.int32, (cp, nr), 1)
    row_f = lax.broadcasted_iota(jnp.int32, (cp, nr), 0)

    def pack_in(acc, tile, c):
        return jnp.where(lax.div(lane_m, 2) == c, pltpu.roll(tile, 2 * c + 1, 1), acc)

    def pack(pad):
        return lax.fori_loop(
            0, mc, lambda c, acc: pack_in(acc, pad[c + 1], c), jnp.zeros((mt, nr), F32), unroll=2
        )

    wall_rows = wall[...]
    w_hi, w_lo = two_parts(wall_rows)
    wcat[:, 0:nr] = w_hi
    wcat[:, nr:2 * nr] = w_lo
    wcat[:, 2 * nr:3 * nr] = jnp.ones((slots, nr), BF16)

    ucopy.wait()
    xcopy.wait()

    @pl.loop(0, ca)
    def _(a):
        face[0, 0, pl.ds(a, 1), :] = upad[a + 1, 0:1, :]
        face[0, 1, pl.ds(a, 1), :] = upad[a + 1, cp - 1:cp, :]

    mpack[0] = pack(xpad)

    pl.semaphore_wait(barrier, devices - 1)
    first = fluid_copies(upad, 0)
    start(first)
    mcopy = [metal_copies(pad, st) for st, pad in enumerate((xpad, da, db))]
    mcopy.append(metal_copies(da, 3))
    start(mcopy[0])

    chunk = min(512, ca * cp)

    @pl.loop(0, ca * cp // chunk)
    def _(i):
        at = lax.broadcasted_iota(jnp.int32, (chunk, slots), 0) + i * chunk
        hot = jnp.where(at == cell_v[...], 1.0, 0.0).astype(BF16)
        sums = jnp.dot(hot, wcat[...], preferred_element_type=F32)
        base = pl.multiple_of(i * chunk, chunk)
        wsum[pl.ds(base, chunk), :] = sums[:, 0:nr] + sums[:, nr:2 * nr]
        wcnt[pl.ds(base, chunk), :] = sums[:, 2 * nr:3 * nr]

    def edges(pad, st):
        wait_got(fluid_copies(pad, st))

        @pl.when(ax == 0)
        def _():
            pad[0] = pad[1]

        @pl.when(ax == na - 1)
        def _():
            pad[ca + 1] = pad[ca]

        @pl.when(pz == 0)
        def _():
            ph[st, 0] = PHASE_COS * ph[st, 0] + PHASE_SIN * fourier[0]

        @pl.when(pz == npi - 1)
        def _():
            ph[st, 1] = PHASE_COS * ph[st, 1] + PHASE_SIN * fourier[1]

    def rate(pad, st, a):
        temp = pad[a + 1]
        east, west = pad[a + 2], pad[a]
        north = jnp.where(row_f == cp - 1, ph[st, 1, pl.ds(a, 1), :], pltpu.roll(temp, cp - 1, 0))
        south = jnp.where(row_f == 0, ph[st, 0, pl.ds(a, 1), :], pltpu.roll(temp, 1, 0))
        outer = jnp.where(lane_f == nr - 1, temp, pltpu.roll(temp, nr - 1, 1))
        inner = jnp.where(lane_f == 0, temp, pltpu.roll(temp, 1, 1))
        spread = east + west + north + south + outer + inner - 6.0 * temp
        base = pl.multiple_of(a * cp, cp)
        sink = HEAT * (wcnt[pl.ds(base, cp), :] * temp - wsum[pl.ds(base, cp), :])
        return temp, (
            -0.5 * aspeed[a] * (east - west) - 0.5 * pspeed[a] * (north - south) + KAPPA * spread - sink
        )

    edges(upad, 0)

    @pl.loop(0, ca)
    def _(a):
        temp, change = rate(upad, 0, a)
        section = temp + change
        spad[a + 1] = section
        avg[pl.ds(pl.multiple_of(a * cp, cp), cp), :] = 0.5 * (temp + section)
        face[1, 0, pl.ds(a, 1), :] = section[0:1]
        face[1, 1, pl.ds(a, 1), :] = section[cp - 1:cp]

    second = fluid_copies(spad, 1)
    start(second)

    @pl.loop(0, slots // 16)
    def _(i):
        for j in range(16):
            s = i * 16 + j
            rows[pl.ds(s, 1), :] = avg[pl.ds(cell_s[s], 1), :]

    f_hi, f_lo = two_parts(HEAT * (rows[...] - wall[...]))
    fcat[:, 0:nr] = f_hi
    fcat[:, nr:2 * nr] = f_lo

    send_chunk = min(512, devices * cap)
    owners = send_chunk // cap

    @pl.loop(0, devices * cap // send_chunk)
    def _(i):
        at = lax.broadcasted_iota(jnp.int32, (send_chunk, slots), 0) + i * send_chunk
        hot = jnp.where(at == key_v[...], 1.0, 0.0).astype(BF16)
        sums = jnp.dot(hot, fcat[...], preferred_element_type=F32)
        part = (sums[:, 0:nr] + sums[:, nr:2 * nr]).reshape(owners, cap, nr)
        snd[pl.ds(i * owners, owners), 0:cap, :] = part
        snd[pl.ds(i * owners, owners), cap:cap + 8, :] = ids_v[pl.ds(i * owners, owners)]

    def out_copy(o):
        e = lax.rem(me + o, devices)
        return remote(snd.at[e], rcv.at[me], asend.at[0, o], arecv.at[0, o], dev(e))

    def in_copy(o):
        e = lax.rem(me - o + devices, devices)
        return remote(snd.at[e], rcv.at[e], asend.at[0, o], arecv.at[0, o], dev(e))

    @pl.loop(1, devices)
    def _(o):
        out_copy(o).start()

    rcv[me] = snd[me]

    def spans(st):
        wait_got(mcopy[st])
        lower = jnp.where(has_lo, pltpu.roll(mh[st, 2], 1, 1), 0.0)
        upper = jnp.where(has_hi, pltpu.roll(mh[st, 3], nr - 1, 1), 0.0)
        return jnp.where(lax.rem(lane_m, 2) == 0, upper, lower)

    def ends(pad, st):
        @pl.when(has_dn)
        def _():
            pad[0] = mh[st, 0]

        @pl.when(has_up)
        def _():
            pad[mc + 1] = mh[st, 1]

    def beside(pad, comb, c):
        tile = pad[c + 1]
        edge = pltpu.roll(comb, nr - 1 - 2 * c, 1)
        total = pad[c] + pad[c + 2]
        total = total + jnp.where(row_m == 0, 0.0, pltpu.roll(tile, 1, 0))
        total = total + jnp.where(row_m == mt - 1, 0.0, pltpu.roll(tile, mt - 1, 0))
        total = total + jnp.where(lane_m == 0, edge, pltpu.roll(tile, 1, 1))
        return tile, total + jnp.where(lane_m == nr - 1, edge, pltpu.roll(tile, nr - 1, 1))

    zero = jnp.zeros((mt, nr), F32)
    for pad in (xpad, da, db):
        pad[0] = zero
        pad[mc + 1] = zero

    comb = spans(0)
    ends(xpad, 0)

    @pl.loop(0, mc)
    def _(c):
        tile, around = beside(xpad, comb, c)
        start_res = around - 6.0 * tile
        res[c] = start_res
        da[c + 1] = start_res * (1.0 / THETA)

    edges(spad, 1)

    @pl.loop(0, ca)
    def _(a):
        temp, change = rate(spad, 1, a)
        fluid_out[a] = avg[pl.ds(pl.multiple_of(a * cp, cp), cp), :] + 0.5 * change

    @pl.loop(1, devices)
    def _(o):
        in_copy(o).wait_recv()

    lane_p = lax.broadcasted_iota(jnp.int32, (8, nr), 1)
    row_p = lax.broadcasted_iota(jnp.int32, (2 * mc, nr), 0).astype(F32) + 1.0

    def place(g):
        ids = rcv[g * group, cap:cap + 8, :]
        for j in range(1, group):
            ids = jnp.where(lax.div(lane_p, cap) == j, rcv[g * group + j, cap:cap + 8, :], ids)
        return jnp.where(row_p == ids[0:1], 1.0, 0.0)

    def gather_in(g, total):
        part = rcv[pl.ds(g * group, group), 0:cap, :].reshape(nr, nr)
        p_hi, p_lo = two_parts(part)
        hot = place(g).astype(BF16)
        return total + (
            jnp.dot(hot, p_hi, preferred_element_type=F32)
            + jnp.dot(hot, p_lo, preferred_element_type=F32)
        )

    inj[...] = lax.fori_loop(0, devices // group, gather_in, jnp.zeros((2 * mc, nr), F32), unroll=4)

    row_e = lax.broadcasted_iota(jnp.int32, (8, nr), 0)

    @pl.loop(0, mc)
    def _(c):
        low = jnp.where(row_e == 0, inj[pl.ds(2 * c, 1), :], 0.0)
        high = jnp.where(row_e == 7, inj[pl.ds(2 * c + 1, 1), :], 0.0)
        res[c, 0:8, :] = res[c, 0:8, :] + low
        res[c, mt - 8:mt, :] = res[c, mt - 8:mt, :] + high
        da[c + 1, 0:8, :] = da[c + 1, 0:8, :] + low * (1.0 / THETA)
        da[c + 1, mt - 8:mt, :] = da[c + 1, mt - 8:mt, :] + high * (1.0 / THETA)

    mpack[1] = pack(da)
    start(mcopy[1])

    factors = cheb_factors()
    for sweep, (old, new) in enumerate(((da, db), (db, da))):
        st = sweep + 1
        comb = spans(st)
        ends(old, st)
        if sweep == 1:
            wait_sent(mcopy[1])
        f0, f1 = factors[sweep]

        def step(c, acc, old=old, new=new, comb=comb, f0=f0, f1=f1, sweep=sweep):
            tile, around = beside(old, comb, c)
            base = xpad[c + 1] if sweep == 0 else metal_out[c]
            metal_out[c] = base + tile
            left = res[c] - ((6.0 + diag[c]) * tile - around)
            res[c] = left
            fresh = f0 * tile + f1 * left
            new[c + 1] = fresh
            return pack_in(acc, fresh, c)

        mpack[st + 1] = lax.fori_loop(0, mc, step, jnp.zeros((mt, nr), F32))
        start(mcopy[st + 1])

    comb = spans(3)
    ends(da, 3)
    f0, f1 = factors[2]

    @pl.loop(0, mc)
    def _(c):
        tile, around = beside(da, comb, c)
        left = res[c] - ((6.0 + diag[c]) * tile - around)
        done = metal_out[c] + tile + (f0 * tile + f1 * left)
        metal_out[c] = done
        inj[pl.ds(2 * c, 1), :] = done[0:1]
        inj[pl.ds(2 * c + 1, 1), :] = done[mt - 1:mt]

    b_hi, b_lo = two_parts(inj[...])
    bcat = jnp.concatenate([b_hi, b_lo], axis=1)

    @pl.loop(0, devices // group)
    def _(g):
        hot = place(g).T.astype(BF16)
        sums = jnp.dot(hot, bcat, preferred_element_type=F32)
        bsnd[pl.ds(pl.multiple_of(g * nr, nr), nr), :] = sums[:, 0:nr] + sums[:, nr:2 * nr]

    def block(ref, e):
        return ref.at[pl.ds(pl.multiple_of(e * cap, cap), cap)]

    def back_out(o):
        e = lax.rem(me + o, devices)
        return remote(block(bsnd, e), block(brcv, me), asend.at[1, o], arecv.at[1, o], dev(e))

    def back_in(o):
        e = lax.rem(me - o + devices, devices)
        return remote(block(bsnd, e), block(brcv, e), asend.at[1, o], arecv.at[1, o], dev(e))

    @pl.loop(1, devices)
    def _(o):
        back_out(o).start()

    own = pl.ds(pl.multiple_of(me * cap, cap), cap)
    brcv[own, :] = bsnd[own, :]

    wait_sent(first)
    wait_sent(second)
    wait_sent(mcopy[0])
    wait_sent(mcopy[2])
    wait_sent(mcopy[3])

    @pl.loop(1, devices)
    def _(o):
        out_copy(o).wait_send()

    @pl.loop(1, devices)
    def _(o):
        back_in(o).wait_recv()

    @pl.loop(0, slots // 16)
    def _(i):
        for j in range(16):
            s = i * 16 + j
            rows[pl.ds(s, 1), :] = brcv[pl.ds(key_s[s], 1), :]

    live = lax.broadcasted_iota(jnp.int32, (slots, nr), 0) < count_s[0]
    wall_out[...] = jnp.where(live, 0.5 * (wall[...] + rows[...]), wall[...])

    @pl.loop(1, devices)
    def _(o):
        back_out(o).wait_send()


def on_device(
    na, npi,
    fluid_temp, axial_speed, pitch_speed, fourier_store, wall_temp, wall_cell,
    wall_owner, wall_target, wall_count, metal_temp, metal_diag,
):
    devices = na * npi
    slots = wall_temp.shape[0]
    ca, cp, nr = fluid_temp.shape
    mc, mt, _ = metal_temp.shape
    cap = max(2, 2 * slots // devices)
    order = jnp.arange(slots, dtype=jnp.int32)
    live = order < wall_count[0]
    owner = wall_owner[:, 0]
    earlier = (owner[:, None] == owner[None, :]) & live[None, :] & (order[None, :] < order[:, None])
    rank = jnp.sum(earlier.astype(jnp.int32), axis=1)
    key = jnp.where(live, owner * cap + rank, -1)
    spots = jnp.arange(devices * cap, dtype=jnp.int32)
    ids = jnp.sum(
        jnp.where(spots[:, None] == key[None, :], (wall_target + 1).astype(F32)[None, :], 0.0), axis=1
    ).reshape(devices, 1, 1, cap)
    ids = jnp.broadcast_to(ids, (devices, 8, nr // cap, cap)).reshape(devices, 8, nr)
    cell_row = jnp.where(live, wall_cell, -1)[None, :]
    vmem = pl.BlockSpec(memory_space=pltpu.VMEM)
    smem = pl.BlockSpec(memory_space=pltpu.SMEM)
    hbm = pl.BlockSpec(memory_space=pl.ANY)
    dma = pltpu.SemaphoreType.DMA
    return pl.pallas_call(
        functools.partial(kernel, na, npi, cap),
        out_shape=(
            jax.ShapeDtypeStruct((ca, cp, nr), F32),
            jax.ShapeDtypeStruct((mc, mt, nr), F32),
            jax.ShapeDtypeStruct((slots, nr), F32),
        ),
        in_specs=[smem] * 3 + [vmem] * 8 + [hbm] * 2,
        out_specs=(vmem, vmem, vmem),
        scratch_shapes=[
            pltpu.VMEM((ca + 2, cp, nr), F32),
            pltpu.VMEM((ca + 2, cp, nr), F32),
            pltpu.VMEM((ca * cp, nr), F32),
            pltpu.VMEM((ca * cp, nr), F32),
            pltpu.VMEM((ca * cp, nr), F32),
            pltpu.VMEM((2, 2, ca, nr), F32),
            pltpu.VMEM((2, 2, ca, nr), F32),
            pltpu.VMEM((slots, 3 * nr), BF16),
            pltpu.VMEM((slots, nr), F32),
            pltpu.VMEM((slots, 2 * nr), BF16),
            pltpu.VMEM((mc + 2, mt, nr), F32),
            pltpu.VMEM((mc + 2, mt, nr), F32),
            pltpu.VMEM((mc + 2, mt, nr), F32),
            pltpu.VMEM((mc, mt, nr), F32),
            pltpu.VMEM((4, 4, mt, nr), F32),
            pltpu.VMEM((4, mt, nr), F32),
            pltpu.VMEM((2 * mc, nr), F32),
            pltpu.VMEM((devices, cap + 8, nr), F32),
            pltpu.VMEM((devices, cap + 8, nr), F32),
            pltpu.VMEM((devices * cap, nr), F32),
            pltpu.VMEM((devices * cap, nr), F32),
            dma((2,)),
            dma((2, 4)),
            dma((2, 4)),
            dma((4, 4)),
            dma((4, 4)),
            dma((2, devices)),
            dma((2, devices)),
        ],
        compiler_params=pltpu.CompilerParams(
            collective_id=0, has_side_effects=True, vmem_limit_bytes=56 * 1024 * 1024
        ),
        name="window",
    )(
        wall_cell, jnp.maximum(key, 0), wall_count,
        cell_row, key[None, :], ids, wall_temp, fourier_store, axial_speed, pitch_speed,
        metal_diag, fluid_temp, metal_temp,
    )


def solution(mesh):
    placed = (
        P("axial", "pitch", None),
        P("axial", "pitch", None),
        P("axial", "pitch", None),
        P(None, "axial", None),
        P(("axial", "pitch"), None),
        P(("axial", "pitch")),
        P(("axial", "pitch"), None),
        P(("axial", "pitch")),
        P(("axial", "pitch")),
        P("axial", None, "pitch"),
        P("axial", None, "pitch"),
    )
    return jax.shard_map(
        functools.partial(on_device, mesh.shape["axial"], mesh.shape["pitch"]),
        mesh=mesh,
        in_specs=placed,
        out_specs=(
            P("axial", "pitch", None),
            P("axial", None, "pitch"),
            P(("axial", "pitch"), None),
        ),
        check_vma=False,
    )
```

```python
import functools

import jax
import jax.numpy as jnp
from jax import lax
from jax.experimental import pallas as pl
from jax.experimental.pallas import tpu as pltpu
from jax.sharding import PartitionSpec as P

SWEEPS = 4
KAPPA = 0.1
HEAT = 0.3
PHASE_COS = 0.8
PHASE_SIN = 0.6
LOW_BOUND = 0.5
HIGH_BOUND = 14.0
THETA = 0.5 * (HIGH_BOUND + LOW_BOUND)
DELTA = 0.5 * (HIGH_BOUND - LOW_BOUND)
MESH = pl.DeviceIdType.MESH
F32 = jnp.float32
BF16 = jnp.bfloat16


def cheb_factors():
    ratio = THETA / DELTA
    rho = 1.0 / ratio
    factors = []
    for _ in range(SWEEPS - 1):
        rho_new = 1.0 / (2.0 * ratio - rho)
        factors.append((rho_new * rho, 2.0 * rho_new / DELTA))
        rho = rho_new
    return factors


def two_parts(value):
    hi = value.astype(BF16)
    lo = (value - hi.astype(F32)).astype(BF16)
    return hi, lo


def kernel(
    na, npi, cap,
    cell_s, key_s, count_s,
    cell_v, key_v, ids_v, wall, fourier, aspeed, pspeed, diag, fluid_hbm, metal_hbm,
    fluid_out, metal_out, wall_out,
    upad, spad, avg, wsum, wcnt, face, ph, wcat, rows, fcat,
    xpad, da, db, res, mh, mpack, inj,
    snd, rcv, bsnd, brcv, part_snd, part_rcv, bound,
    lsem, fsend, frecv, msend, mrecv, asend, arecv, psend, precv,
):
    ax = lax.axis_index("axial")
    pz = lax.axis_index("pitch")
    devices = na * npi
    ca, cp, nr = aspeed.shape
    mc, mt, _ = diag.shape
    slots = wall.shape[0]
    group = nr // cap

    up_axial = (jnp.minimum(ax + 1, na - 1), pz)
    dn_axial = (jnp.maximum(ax - 1, 0), pz)
    north_dev = (ax, lax.rem(pz + 1, npi))
    south_dev = (ax, lax.rem(pz + npi - 1, npi))
    has_dn, has_up = ax > 0, ax < na - 1
    has_lo, has_hi = pz > 0, pz < npi - 1

    ucopy = pltpu.make_async_copy(fluid_hbm, upad.at[pl.ds(1, ca)], lsem.at[0])
    xcopy = pltpu.make_async_copy(metal_hbm, xpad.at[pl.ds(1, mc)], lsem.at[1])
    ucopy.start()
    xcopy.start()

    barrier = pltpu.get_barrier_semaphore()

    def axial_peer(o):
        return lax.rem(ax + o, na)

    def pitch_peer(o):
        return lax.rem(pz + o, npi)

    for o in range(1, na):
        pl.semaphore_signal(barrier, inc=1, device_id=(axial_peer(o), pz), device_id_type=MESH)
    for o in range(1, npi):
        pl.semaphore_signal(barrier, inc=1, device_id=(ax, pitch_peer(o)), device_id_type=MESH)

    def remote(src, dst, ssem, rsem, device):
        return pltpu.make_async_remote_copy(
            src_ref=src, dst_ref=dst, send_sem=ssem, recv_sem=rsem,
            device_id=device, device_id_type=MESH,
        )

    def fluid_copies(pad, st):
        return (
            (has_up, has_dn, remote(pad.at[ca], pad.at[0], fsend.at[st, 0], frecv.at[st, 0], up_axial)),
            (has_dn, has_up, remote(pad.at[1], pad.at[ca + 1], fsend.at[st, 1], frecv.at[st, 1], dn_axial)),
            (None, None, remote(face.at[st, 1], ph.at[st, 0], fsend.at[st, 2], frecv.at[st, 2], north_dev)),
            (None, None, remote(face.at[st, 0], ph.at[st, 1], fsend.at[st, 3], frecv.at[st, 3], south_dev)),
        )

    def metal_copies(pad, st):
        return (
            (has_up, has_dn, remote(pad.at[mc], mh.at[st, 0], msend.at[st, 0], mrecv.at[st, 0], up_axial)),
            (has_dn, has_up, remote(pad.at[1], mh.at[st, 1], msend.at[st, 1], mrecv.at[st, 1], dn_axial)),
            (has_hi, has_lo, remote(mpack.at[st], mh.at[st, 2], msend.at[st, 2], mrecv.at[st, 2], north_dev)),
            (has_lo, has_hi, remote(mpack.at[st], mh.at[st, 3], msend.at[st, 3], mrecv.at[st, 3], south_dev)),
        )

    def when(condition, action):
        if condition is None:
            action()
        else:
            pl.when(condition)(action)

    def start(copies):
        for sends, _, copy in copies:
            when(sends, copy.start)

    def wait_sent(copies):
        for sends, _, copy in copies:
            when(sends, copy.wait_send)

    def wait_got(copies):
        for _, gets, copy in copies:
            when(gets, copy.wait_recv)

    lane_m = lax.broadcasted_iota(jnp.int32, (mt, nr), 1)
    row_m = lax.broadcasted_iota(jnp.int32, (mt, nr), 0)
    lane_f = lax.broadcasted_iota(jnp.int32, (cp, nr), 1)
    row_f = lax.broadcasted_iota(jnp.int32, (cp, nr), 0)

    def pack_in(acc, tile, c):
        return jnp.where(lax.div(lane_m, 2) == c, pltpu.roll(tile, 2 * c + 1, 1), acc)

    def pack(pad):
        return lax.fori_loop(
            0, mc, lambda c, acc: pack_in(acc, pad[c + 1], c), jnp.zeros((mt, nr), F32), unroll=8
        )

    wall_rows = wall[...]
    w_hi, w_lo = two_parts(wall_rows)
    wcat[:, 0:nr] = w_hi
    wcat[:, nr:2 * nr] = w_lo
    wcat[:, 2 * nr:3 * nr] = jnp.ones((slots, nr), BF16)

    ucopy.wait()
    xcopy.wait()

    @pl.loop(0, ca, unroll=2)
    def _(a):
        face[0, 0, pl.ds(a, 1), :] = upad[a + 1, 0:1, :]
        face[0, 1, pl.ds(a, 1), :] = upad[a + 1, cp - 1:cp, :]

    mpack[0] = pack(xpad)

    pl.semaphore_wait(barrier, na + npi - 2)
    first = fluid_copies(upad, 0)
    start(first)
    mcopy = [metal_copies(pad, st) for st, pad in enumerate((xpad, da, db))]
    mcopy.append(metal_copies(da, 3))
    start(mcopy[0])

    chunk = min(512, ca * cp)

    @pl.loop(0, ca * cp // chunk)
    def _(i):
        at = lax.broadcasted_iota(jnp.int32, (chunk, slots), 0) + i * chunk
        hot = jnp.where(at == cell_v[...], 1.0, 0.0).astype(BF16)
        sums = jnp.dot(hot, wcat[...], preferred_element_type=F32)
        base = pl.multiple_of(i * chunk, chunk)
        wsum[pl.ds(base, chunk), :] = sums[:, 0:nr] + sums[:, nr:2 * nr]
        wcnt[pl.ds(base, chunk), :] = sums[:, 2 * nr:3 * nr]

    def edges(pad, st):
        wait_got(fluid_copies(pad, st))

        @pl.when(ax == 0)
        def _():
            pad[0] = pad[1]

        @pl.when(ax == na - 1)
        def _():
            pad[ca + 1] = pad[ca]

        @pl.when(pz == 0)
        def _():
            ph[st, 0] = PHASE_COS * ph[st, 0] + PHASE_SIN * fourier[0]

        @pl.when(pz == npi - 1)
        def _():
            ph[st, 1] = PHASE_COS * ph[st, 1] + PHASE_SIN * fourier[1]

    def rate(pad, st, a):
        temp = pad[a + 1]
        east, west = pad[a + 2], pad[a]
        north = jnp.where(row_f == cp - 1, ph[st, 1, pl.ds(a, 1), :], pltpu.roll(temp, cp - 1, 0))
        south = jnp.where(row_f == 0, ph[st, 0, pl.ds(a, 1), :], pltpu.roll(temp, 1, 0))
        outer = jnp.where(lane_f == nr - 1, temp, pltpu.roll(temp, nr - 1, 1))
        inner = jnp.where(lane_f == 0, temp, pltpu.roll(temp, 1, 1))
        spread = east + west + north + south + outer + inner - 6.0 * temp
        base = pl.multiple_of(a * cp, cp)
        sink = HEAT * (wcnt[pl.ds(base, cp), :] * temp - wsum[pl.ds(base, cp), :])
        return temp, (
            -0.5 * aspeed[a] * (east - west) - 0.5 * pspeed[a] * (north - south) + KAPPA * spread - sink
        )

    edges(upad, 0)

    @pl.loop(0, ca, unroll=2)
    def _(a):
        temp, change = rate(upad, 0, a)
        section = temp + change
        spad[a + 1] = section
        avg[pl.ds(pl.multiple_of(a * cp, cp), cp), :] = 0.5 * (temp + section)
        face[1, 0, pl.ds(a, 1), :] = section[0:1]
        face[1, 1, pl.ds(a, 1), :] = section[cp - 1:cp]

    second = fluid_copies(spad, 1)
    start(second)

    @pl.loop(0, slots // 16)
    def _(i):
        for j in range(16):
            s = i * 16 + j
            rows[pl.ds(s, 1), :] = avg[pl.ds(cell_s[s], 1), :]

    f_hi, f_lo = two_parts(HEAT * (rows[...] - wall[...]))
    fcat[:, 0:nr] = f_hi
    fcat[:, nr:2 * nr] = f_lo

    send_chunk = min(512, devices * cap)
    owners = send_chunk // cap

    @pl.loop(0, devices * cap // send_chunk)
    def _(i):
        at = lax.broadcasted_iota(jnp.int32, (send_chunk, slots), 0) + i * send_chunk
        hot = jnp.where(at == key_v[...], 1.0, 0.0).astype(BF16)
        sums = jnp.dot(hot, fcat[...], preferred_element_type=F32)
        part = (sums[:, 0:nr] + sums[:, nr:2 * nr]).reshape(owners, cap, nr)
        snd[pl.ds(i * owners, owners), 0:cap, :] = part
        snd[pl.ds(i * owners, owners), cap:cap + 8, :] = ids_v[pl.ds(i * owners, owners)]

    def out_copy(o, j):
        return remote(
            snd.at[pl.ds(j * npi, npi)], rcv.at[pl.ds(ax * npi, npi)], asend.at[0, o], arecv.at[0, o],
            (axial_peer(o), pz),
        )

    def in_copy(o):
        i = lax.rem(ax - o + na, na)
        return remote(
            snd.at[pl.ds(i * npi, npi)], rcv.at[pl.ds(i * npi, npi)], asend.at[0, o], arecv.at[0, o],
            (i, pz),
        )

    for o in range(1, na):
        out_copy(o, axial_peer(o)).start()

    rcv[pl.ds(ax * npi, npi)] = snd[pl.ds(ax * npi, npi)]

    def spans(st):
        wait_got(mcopy[st])
        lower = jnp.where(has_lo, pltpu.roll(mh[st, 2], 1, 1), 0.0)
        upper = jnp.where(has_hi, pltpu.roll(mh[st, 3], nr - 1, 1), 0.0)
        return jnp.where(lax.rem(lane_m, 2) == 0, upper, lower)

    def ends(pad, st):
        @pl.when(has_dn)
        def _():
            pad[0] = mh[st, 0]

        @pl.when(has_up)
        def _():
            pad[mc + 1] = mh[st, 1]

    def beside(pad, comb, c):
        tile = pad[c + 1]
        edge = pltpu.roll(comb, nr - 1 - 2 * c, 1)
        total = pad[c] + pad[c + 2]
        total = total + jnp.where(row_m == 0, 0.0, pltpu.roll(tile, 1, 0))
        total = total + jnp.where(row_m == mt - 1, 0.0, pltpu.roll(tile, mt - 1, 0))
        total = total + jnp.where(lane_m == 0, edge, pltpu.roll(tile, 1, 1))
        return tile, total + jnp.where(lane_m == nr - 1, edge, pltpu.roll(tile, nr - 1, 1))

    zero = jnp.zeros((mt, nr), F32)
    for pad in (xpad, da, db):
        pad[0] = zero
        pad[mc + 1] = zero

    comb = spans(0)
    ends(xpad, 0)

    @pl.loop(0, mc, unroll=4)
    def _(c):
        tile, around = beside(xpad, comb, c)
        start_res = around - 6.0 * tile
        res[c] = start_res
        da[c + 1] = start_res * (1.0 / THETA)

    edges(spad, 1)

    @pl.loop(0, ca, unroll=2)
    def _(a):
        temp, change = rate(spad, 1, a)
        fluid_out[a] = avg[pl.ds(pl.multiple_of(a * cp, cp), cp), :] + 0.5 * change

    for o in range(1, na):
        in_copy(o).wait_recv()

    lane_p = lax.broadcasted_iota(jnp.int32, (8, nr), 1)
    row_p = lax.broadcasted_iota(jnp.int32, (2 * mc, nr), 0).astype(F32) + 1.0
    span = min(group, na)
    width = span * cap

    def place(g, z):
        ids = rcv[g * span * npi + z, cap:cap + 8, :]
        for j in range(1, span):
            ids = jnp.where(
                lax.div(lane_p, cap) == j, rcv[(g * span + j) * npi + z, cap:cap + 8, :], ids
            )
        return jnp.where(row_p[:, 0:width] == ids[0:1, 0:width], 1.0, 0.0)

    def injected(z):
        def gather_in(g, total):
            part = jnp.concatenate(
                [rcv[(g * span + j) * npi + z, 0:cap, :] for j in range(span)], axis=0
            )
            p_hi, p_lo = two_parts(part)
            hot = place(g, z).astype(BF16)
            return total + (
                jnp.dot(hot, p_hi, preferred_element_type=F32)
                + jnp.dot(hot, p_lo, preferred_element_type=F32)
            )

        total = jnp.zeros((2 * mc, nr), F32)
        for g in range(na // span):
            total = gather_in(g, total)
        return total

    def part_out(o):
        return remote(
            part_snd.at[o], part_rcv.at[o], psend.at[0, o], precv.at[0, o], (ax, pitch_peer(o))
        )

    for o in range(1, npi):
        part_snd[o] = injected(pitch_peer(o))
        part_out(o).start()
    mine = injected(pz)
    for o in range(1, npi):
        part_out(o).wait_recv()
        mine = mine + part_rcv[o]
    inj[...] = mine

    row_e = lax.broadcasted_iota(jnp.int32, (8, nr), 0)

    @pl.loop(0, mc, unroll=4)
    def _(c):
        low = jnp.where(row_e == 0, inj[pl.ds(2 * c, 1), :], 0.0)
        high = jnp.where(row_e == 7, inj[pl.ds(2 * c + 1, 1), :], 0.0)
        res[c, 0:8, :] = res[c, 0:8, :] + low
        res[c, mt - 8:mt, :] = res[c, mt - 8:mt, :] + high
        da[c + 1, 0:8, :] = da[c + 1, 0:8, :] + low * (1.0 / THETA)
        da[c + 1, mt - 8:mt, :] = da[c + 1, mt - 8:mt, :] + high * (1.0 / THETA)

    mpack[1] = pack(da)
    start(mcopy[1])

    factors = cheb_factors()
    for sweep, (old, new) in enumerate(((da, db), (db, da))):
        st = sweep + 1
        comb = spans(st)
        ends(old, st)
        if sweep == 1:
            wait_sent(mcopy[1])
        f0, f1 = factors[sweep]

        def step(c, acc, old=old, new=new, comb=comb, f0=f0, f1=f1, sweep=sweep):
            tile, around = beside(old, comb, c)
            base = xpad[c + 1] if sweep == 0 else metal_out[c]
            metal_out[c] = base + tile
            left = res[c] - ((6.0 + diag[c]) * tile - around)
            res[c] = left
            fresh = f0 * tile + f1 * left
            new[c + 1] = fresh
            return pack_in(acc, fresh, c)

        mpack[st + 1] = lax.fori_loop(0, mc, step, jnp.zeros((mt, nr), F32), unroll=4)
        start(mcopy[st + 1])

    comb = spans(3)
    ends(da, 3)
    f0, f1 = factors[2]

    @pl.loop(0, mc, unroll=4)
    def _(c):
        tile, around = beside(da, comb, c)
        left = res[c] - ((6.0 + diag[c]) * tile - around)
        done = metal_out[c] + tile + (f0 * tile + f1 * left)
        metal_out[c] = done
        inj[pl.ds(2 * c, 1), :] = done[0:1]
        inj[pl.ds(2 * c + 1, 1), :] = done[mt - 1:mt]

    bound[0] = inj[...]

    def bound_out(o):
        return remote(
            bound.at[0], bound.at[o], psend.at[1, o], precv.at[1, o], (ax, pitch_peer(o))
        )

    for o in range(1, npi):
        bound_out(o).start()

    for o in range(npi):
        z = lax.rem(pz - o + npi, npi)
        if o:
            bound_out(o).wait_recv()
        b_hi, b_lo = two_parts(bound[o])
        bcat = jnp.concatenate([b_hi, b_lo], axis=1)
        for g in range(na // span):
            hot = place(g, z).T.astype(BF16)
            sums = jnp.dot(hot, bcat, preferred_element_type=F32)
            sums = sums[:, 0:nr] + sums[:, nr:2 * nr]
            for j in range(span):
                at = pl.multiple_of(((g * span + j) * npi + z) * cap, cap)
                bsnd[pl.ds(at, cap), :] = sums[j * cap:(j + 1) * cap]

    def block(ref, i):
        return ref.at[pl.ds(pl.multiple_of(i * npi * cap, npi * cap), npi * cap)]

    def back_out(o):
        return remote(
            block(bsnd, axial_peer(o)), block(brcv, ax), asend.at[1, o], arecv.at[1, o],
            (axial_peer(o), pz),
        )

    def back_in(o):
        i = lax.rem(ax - o + na, na)
        return remote(block(bsnd, i), block(brcv, i), asend.at[1, o], arecv.at[1, o], (i, pz))

    for o in range(1, na):
        back_out(o).start()

    own = pl.ds(pl.multiple_of(ax * npi * cap, npi * cap), npi * cap)
    brcv[own, :] = bsnd[own, :]

    wait_sent(first)
    wait_sent(second)
    wait_sent(mcopy[0])
    wait_sent(mcopy[2])
    wait_sent(mcopy[3])
    for o in range(1, na):
        out_copy(o, axial_peer(o)).wait_send()
    for o in range(1, npi):
        part_out(o).wait_send()
        bound_out(o).wait_send()
    for o in range(1, na):
        back_in(o).wait_recv()

    @pl.loop(0, slots // 16)
    def _(i):
        for j in range(16):
            s = i * 16 + j
            rows[pl.ds(s, 1), :] = brcv[pl.ds(key_s[s], 1), :]

    live = lax.broadcasted_iota(jnp.int32, (slots, nr), 0) < count_s[0]
    wall_out[...] = jnp.where(live, 0.5 * (wall[...] + rows[...]), wall[...])

    for o in range(1, na):
        back_out(o).wait_send()


def on_device(
    na, npi,
    fluid_temp, axial_speed, pitch_speed, fourier_store, wall_temp, wall_cell,
    wall_owner, wall_target, wall_count, metal_temp, metal_diag,
):
    devices = na * npi
    slots = wall_temp.shape[0]
    ca, cp, nr = fluid_temp.shape
    mc, mt, _ = metal_temp.shape
    cap = max(2, 2 * slots // devices)
    order = jnp.arange(slots, dtype=jnp.int32)
    live = order < wall_count[0]
    owner = wall_owner[:, 0]
    earlier = (owner[:, None] == owner[None, :]) & live[None, :] & (order[None, :] < order[:, None])
    rank = jnp.sum(earlier.astype(jnp.int32), axis=1)
    key = jnp.where(live, owner * cap + rank, -1)
    spots = jnp.arange(devices * cap, dtype=jnp.int32)
    ids = jnp.sum(
        jnp.where(spots[:, None] == key[None, :], (wall_target + 1).astype(F32)[None, :], 0.0), axis=1
    ).reshape(devices, 1, 1, cap)
    ids = jnp.broadcast_to(ids, (devices, 8, nr // cap, cap)).reshape(devices, 8, nr)
    cell_row = jnp.where(live, wall_cell, -1)[None, :]
    vmem = pl.BlockSpec(memory_space=pltpu.VMEM)
    smem = pl.BlockSpec(memory_space=pltpu.SMEM)
    hbm = pl.BlockSpec(memory_space=pl.ANY)
    dma = pltpu.SemaphoreType.DMA
    return pl.pallas_call(
        functools.partial(kernel, na, npi, cap),
        out_shape=(
            jax.ShapeDtypeStruct((ca, cp, nr), F32),
            jax.ShapeDtypeStruct((mc, mt, nr), F32),
            jax.ShapeDtypeStruct((slots, nr), F32),
        ),
        in_specs=[smem] * 3 + [vmem] * 8 + [hbm] * 2,
        out_specs=(vmem, vmem, vmem),
        scratch_shapes=[
            pltpu.VMEM((ca + 2, cp, nr), F32),
            pltpu.VMEM((ca + 2, cp, nr), F32),
            pltpu.VMEM((ca * cp, nr), F32),
            pltpu.VMEM((ca * cp, nr), F32),
            pltpu.VMEM((ca * cp, nr), F32),
            pltpu.VMEM((2, 2, ca, nr), F32),
            pltpu.VMEM((2, 2, ca, nr), F32),
            pltpu.VMEM((slots, 3 * nr), BF16),
            pltpu.VMEM((slots, nr), F32),
            pltpu.VMEM((slots, 2 * nr), BF16),
            pltpu.VMEM((mc + 2, mt, nr), F32),
            pltpu.VMEM((mc + 2, mt, nr), F32),
            pltpu.VMEM((mc + 2, mt, nr), F32),
            pltpu.VMEM((mc, mt, nr), F32),
            pltpu.VMEM((4, 4, mt, nr), F32),
            pltpu.VMEM((4, mt, nr), F32),
            pltpu.VMEM((2 * mc, nr), F32),
            pltpu.VMEM((devices, cap + 8, nr), F32),
            pltpu.VMEM((devices, cap + 8, nr), F32),
            pltpu.VMEM((devices * cap, nr), F32),
            pltpu.VMEM((devices * cap, nr), F32),
            pltpu.VMEM((npi, 2 * mc, nr), F32),
            pltpu.VMEM((npi, 2 * mc, nr), F32),
            pltpu.VMEM((npi, 2 * mc, nr), F32),
            dma((2,)),
            dma((2, 4)),
            dma((2, 4)),
            dma((4, 4)),
            dma((4, 4)),
            dma((2, na)),
            dma((2, na)),
            dma((2, npi)),
            dma((2, npi)),
        ],
        compiler_params=pltpu.CompilerParams(
            collective_id=0, has_side_effects=True, vmem_limit_bytes=56 * 1024 * 1024
        ),
        name="window",
    )(
        wall_cell, jnp.maximum(key, 0), wall_count,
        cell_row, key[None, :], ids, wall_temp, fourier_store, axial_speed, pitch_speed,
        metal_diag, fluid_temp, metal_temp,
    )


def solution(mesh):
    placed = (
        P("axial", "pitch", None),
        P("axial", "pitch", None),
        P("axial", "pitch", None),
        P(None, "axial", None),
        P(("axial", "pitch"), None),
        P(("axial", "pitch")),
        P(("axial", "pitch"), None),
        P(("axial", "pitch")),
        P(("axial", "pitch")),
        P("axial", None, "pitch"),
        P("axial", None, "pitch"),
    )
    return jax.shard_map(
        functools.partial(on_device, mesh.shape["axial"], mesh.shape["pitch"]),
        mesh=mesh,
        in_specs=placed,
        out_specs=(
            P("axial", "pitch", None),
            P("axial", None, "pitch"),
            P(("axial", "pitch"), None),
        ),
        check_vma=False,
    )
```

```python
import functools

import jax
import jax.numpy as jnp
from jax import lax
from jax.experimental import pallas as pl
from jax.experimental.pallas import tpu as pltpu
from jax.sharding import PartitionSpec as P

SWEEPS = 4
KAPPA = 0.1
HEAT = 0.3
PHASE_COS = 0.8
PHASE_SIN = 0.6
LOW_BOUND = 0.5
HIGH_BOUND = 14.0
THETA = 0.5 * (HIGH_BOUND + LOW_BOUND)
DELTA = 0.5 * (HIGH_BOUND - LOW_BOUND)
MESH = pl.DeviceIdType.MESH
F32 = jnp.float32
BF16 = jnp.bfloat16


def cheb_factors():
    ratio = THETA / DELTA
    rho = 1.0 / ratio
    factors = []
    for _ in range(SWEEPS - 1):
        rho_new = 1.0 / (2.0 * ratio - rho)
        factors.append((rho_new * rho, 2.0 * rho_new / DELTA))
        rho = rho_new
    return factors


def two_parts(value):
    hi = value.astype(BF16)
    lo = (value - hi.astype(F32)).astype(BF16)
    return hi, lo


def kernel(
    na, npi, cap,
    cell_s, key_s, count_s,
    cell_v, key_v, ids_v, wall, fourier, aspeed, pspeed, diag, fluid_hbm, metal_hbm,
    fluid_out, metal_out, wall_out,
    upad, spad, avg, wsum, wcnt, face, ph, wcat, rows, fcat,
    xpad, da, db, res, mh, mpack, inj,
    snd, rcv, bsnd, brcv, part_snd, part_rcv, bound,
    lsem, fsend, frecv, msend, mrecv, asend, arecv, psend, precv,
):
    ax = lax.axis_index("axial")
    pz = lax.axis_index("pitch")
    devices = na * npi
    ca, cp, nr = aspeed.shape
    mc, mt, _ = diag.shape
    slots = wall.shape[0]
    group = nr // cap

    up_axial = (jnp.minimum(ax + 1, na - 1), pz)
    dn_axial = (jnp.maximum(ax - 1, 0), pz)
    north_dev = (ax, lax.rem(pz + 1, npi))
    south_dev = (ax, lax.rem(pz + npi - 1, npi))
    has_dn, has_up = ax > 0, ax < na - 1
    has_lo, has_hi = pz > 0, pz < npi - 1

    ucopy = pltpu.make_async_copy(fluid_hbm, upad.at[pl.ds(1, ca)], lsem.at[0])
    xcopy = pltpu.make_async_copy(metal_hbm, xpad.at[pl.ds(1, mc)], lsem.at[1])
    ucopy.start()
    xcopy.start()

    barrier = pltpu.get_barrier_semaphore()

    def axial_peer(o):
        return lax.rem(ax + o, na)

    def pitch_peer(o):
        return lax.rem(pz + o, npi)

    for o in range(1, na):
        pl.semaphore_signal(barrier, inc=1, device_id=(axial_peer(o), pz), device_id_type=MESH)
    for o in range(1, npi):
        pl.semaphore_signal(barrier, inc=1, device_id=(ax, pitch_peer(o)), device_id_type=MESH)

    def remote(src, dst, ssem, rsem, device):
        return pltpu.make_async_remote_copy(
            src_ref=src, dst_ref=dst, send_sem=ssem, recv_sem=rsem,
            device_id=device, device_id_type=MESH,
        )

    def fluid_copies(pad, st):
        return (
            (has_up, has_dn, remote(pad.at[ca], pad.at[0], fsend.at[st, 0], frecv.at[st, 0], up_axial)),
            (has_dn, has_up, remote(pad.at[1], pad.at[ca + 1], fsend.at[st, 1], frecv.at[st, 1], dn_axial)),
            (None, None, remote(face.at[st, 1], ph.at[st, 0], fsend.at[st, 2], frecv.at[st, 2], north_dev)),
            (None, None, remote(face.at[st, 0], ph.at[st, 1], fsend.at[st, 3], frecv.at[st, 3], south_dev)),
        )

    def metal_copies(pad, st):
        return (
            (has_up, has_dn, remote(pad.at[mc], mh.at[st, 0], msend.at[st, 0], mrecv.at[st, 0], up_axial)),
            (has_dn, has_up, remote(pad.at[1], mh.at[st, 1], msend.at[st, 1], mrecv.at[st, 1], dn_axial)),
            (has_hi, has_lo, remote(mpack.at[st], mh.at[st, 2], msend.at[st, 2], mrecv.at[st, 2], north_dev)),
            (has_lo, has_hi, remote(mpack.at[st], mh.at[st, 3], msend.at[st, 3], mrecv.at[st, 3], south_dev)),
        )

    def when(condition, action):
        if condition is None:
            action()
        else:
            pl.when(condition)(action)

    def start(copies):
        for sends, _, copy in copies:
            when(sends, copy.start)

    def wait_sent(copies):
        for sends, _, copy in copies:
            when(sends, copy.wait_send)

    def wait_got(copies):
        for _, gets, copy in copies:
            when(gets, copy.wait_recv)

    lane_m = lax.broadcasted_iota(jnp.int32, (mt, nr), 1)
    row_m = lax.broadcasted_iota(jnp.int32, (mt, nr), 0)
    lane_f = lax.broadcasted_iota(jnp.int32, (cp, nr), 1)
    row_f = lax.broadcasted_iota(jnp.int32, (cp, nr), 0)

    def pack_in(acc, tile, c):
        return jnp.where(lax.div(lane_m, 2) == c, pltpu.roll(tile, 2 * c + 1, 1), acc)

    def pack(pad):
        return lax.fori_loop(
            0, mc, lambda c, acc: pack_in(acc, pad[c + 1], c), jnp.zeros((mt, nr), F32), unroll=8
        )

    wall_rows = wall[...]
    w_hi, w_lo = two_parts(wall_rows)
    wcat[:, 0:nr] = w_hi
    wcat[:, nr:2 * nr] = w_lo
    wcat[:, 2 * nr:3 * nr] = jnp.ones((slots, nr), BF16)

    ucopy.wait()
    xcopy.wait()

    @pl.loop(0, ca, unroll=2)
    def _(a):
        face[0, 0, pl.ds(a, 1), :] = upad[a + 1, 0:1, :]
        face[0, 1, pl.ds(a, 1), :] = upad[a + 1, cp - 1:cp, :]

    mpack[0] = pack(xpad)

    pl.semaphore_wait(barrier, na + npi - 2)
    first = fluid_copies(upad, 0)
    start(first)
    mcopy = [metal_copies(pad, st) for st, pad in enumerate((xpad, da, db))]
    mcopy.append(metal_copies(da, 3))
    start(mcopy[0])

    chunk = min(512, ca * cp)

    @pl.loop(0, ca * cp // chunk)
    def _(i):
        at = lax.broadcasted_iota(jnp.int32, (chunk, slots), 0) + i * chunk
        hot = jnp.where(at == cell_v[...], 1.0, 0.0).astype(BF16)
        sums = jnp.dot(hot, wcat[...], preferred_element_type=F32)
        base = pl.multiple_of(i * chunk, chunk)
        wsum[pl.ds(base, chunk), :] = sums[:, 0:nr] + sums[:, nr:2 * nr]
        wcnt[pl.ds(base, chunk), :] = sums[:, 2 * nr:3 * nr]

    def edges(pad, st):
        wait_got(fluid_copies(pad, st))

        @pl.when(ax == 0)
        def _():
            pad[0] = pad[1]

        @pl.when(ax == na - 1)
        def _():
            pad[ca + 1] = pad[ca]

        @pl.when(pz == 0)
        def _():
            ph[st, 0] = PHASE_COS * ph[st, 0] + PHASE_SIN * fourier[0]

        @pl.when(pz == npi - 1)
        def _():
            ph[st, 1] = PHASE_COS * ph[st, 1] + PHASE_SIN * fourier[1]

    def rate(pad, st, a):
        temp = pad[a + 1]
        east, west = pad[a + 2], pad[a]
        north = jnp.where(row_f == cp - 1, ph[st, 1, pl.ds(a, 1), :], pltpu.roll(temp, cp - 1, 0))
        south = jnp.where(row_f == 0, ph[st, 0, pl.ds(a, 1), :], pltpu.roll(temp, 1, 0))
        outer = jnp.where(lane_f == nr - 1, temp, pltpu.roll(temp, nr - 1, 1))
        inner = jnp.where(lane_f == 0, temp, pltpu.roll(temp, 1, 1))
        spread = east + west + north + south + outer + inner - 6.0 * temp
        base = pl.multiple_of(a * cp, cp)
        sink = HEAT * (wcnt[pl.ds(base, cp), :] * temp - wsum[pl.ds(base, cp), :])
        return temp, (
            -0.5 * aspeed[a] * (east - west) - 0.5 * pspeed[a] * (north - south) + KAPPA * spread - sink
        )

    edges(upad, 0)

    @pl.loop(0, ca, unroll=2)
    def _(a):
        temp, change = rate(upad, 0, a)
        section = temp + change
        spad[a + 1] = section
        avg[pl.ds(pl.multiple_of(a * cp, cp), cp), :] = 0.5 * (temp + section)
        face[1, 0, pl.ds(a, 1), :] = section[0:1]
        face[1, 1, pl.ds(a, 1), :] = section[cp - 1:cp]

    second = fluid_copies(spad, 1)
    start(second)

    @pl.loop(0, slots // 16)
    def _(i):
        for j in range(16):
            s = i * 16 + j
            rows[pl.ds(s, 1), :] = avg[pl.ds(cell_s[s], 1), :]

    f_hi, f_lo = two_parts(HEAT * (rows[...] - wall[...]))
    fcat[:, 0:nr] = f_hi
    fcat[:, nr:2 * nr] = f_lo

    send_chunk = min(512, devices * cap)
    owners = send_chunk // cap

    @pl.loop(0, devices * cap // send_chunk)
    def _(i):
        at = lax.broadcasted_iota(jnp.int32, (send_chunk, slots), 0) + i * send_chunk
        hot = jnp.where(at == key_v[...], 1.0, 0.0).astype(BF16)
        sums = jnp.dot(hot, fcat[...], preferred_element_type=F32)
        part = (sums[:, 0:nr] + sums[:, nr:2 * nr]).reshape(owners, cap, nr)
        snd[pl.ds(i * owners, owners), 0:cap, :] = part
        snd[pl.ds(i * owners, owners), cap:cap + 8, :] = ids_v[pl.ds(i * owners, owners)]

    def out_copy(o, zo):
        i, z = axial_peer(o), pitch_peer(zo)
        return remote(
            snd.at[i * npi + z], rcv.at[ax * npi + z], asend.at[0, zo, o], arecv.at[0, zo, o], (i, pz)
        )

    def in_copy(o, zo):
        i, z = lax.rem(ax - o + na, na), pitch_peer(zo)
        return remote(
            snd.at[i * npi + z], rcv.at[i * npi + z], asend.at[0, zo, o], arecv.at[0, zo, o], (i, pz)
        )

    z_order = tuple(range(1, npi)) + (0,)
    for zo in z_order:

        @pl.loop(1, na)
        def _(o, zo=zo):
            out_copy(o, zo).start()

    rcv[pl.ds(ax * npi, npi)] = snd[pl.ds(ax * npi, npi)]

    def spans(st):
        wait_got(mcopy[st])
        lower = jnp.where(has_lo, pltpu.roll(mh[st, 2], 1, 1), 0.0)
        upper = jnp.where(has_hi, pltpu.roll(mh[st, 3], nr - 1, 1), 0.0)
        return jnp.where(lax.rem(lane_m, 2) == 0, upper, lower)

    def ends(pad, st):
        @pl.when(has_dn)
        def _():
            pad[0] = mh[st, 0]

        @pl.when(has_up)
        def _():
            pad[mc + 1] = mh[st, 1]

    def beside(pad, comb, c):
        tile = pad[c + 1]
        edge = pltpu.roll(comb, nr - 1 - 2 * c, 1)
        total = pad[c] + pad[c + 2]
        total = total + jnp.where(row_m == 0, 0.0, pltpu.roll(tile, 1, 0))
        total = total + jnp.where(row_m == mt - 1, 0.0, pltpu.roll(tile, mt - 1, 0))
        total = total + jnp.where(lane_m == 0, edge, pltpu.roll(tile, 1, 1))
        return tile, total + jnp.where(lane_m == nr - 1, edge, pltpu.roll(tile, nr - 1, 1))

    zero = jnp.zeros((mt, nr), F32)
    for pad in (xpad, da, db):
        pad[0] = zero
        pad[mc + 1] = zero

    comb = spans(0)
    ends(xpad, 0)

    @pl.loop(0, mc, unroll=4)
    def _(c):
        tile, around = beside(xpad, comb, c)
        start_res = around - 6.0 * tile
        res[c] = start_res
        da[c + 1] = start_res * (1.0 / THETA)

    edges(spad, 1)

    @pl.loop(0, ca, unroll=2)
    def _(a):
        temp, change = rate(spad, 1, a)
        fluid_out[a] = avg[pl.ds(pl.multiple_of(a * cp, cp), cp), :] + 0.5 * change

    def got_rows(zo):
        @pl.loop(1, na)
        def _(o):
            in_copy(o, zo).wait_recv()

    lane_p = lax.broadcasted_iota(jnp.int32, (8, nr), 1)
    row_p = lax.broadcasted_iota(jnp.int32, (2 * mc, nr), 0).astype(F32) + 1.0
    span = min(group, na)
    width = span * cap

    def place(g, z):
        ids = rcv[g * span * npi + z, cap:cap + 8, :]
        for j in range(1, span):
            ids = jnp.where(
                lax.div(lane_p, cap) == j, rcv[(g * span + j) * npi + z, cap:cap + 8, :], ids
            )
        return jnp.where(row_p[:, 0:width] == ids[0:1, 0:width], 1.0, 0.0)

    def injected(z):
        def gather_in(g, total):
            part = jnp.concatenate(
                [rcv[(g * span + j) * npi + z, 0:cap, :] for j in range(span)], axis=0
            )
            p_hi, p_lo = two_parts(part)
            hot = place(g, z).astype(BF16)
            return total + (
                jnp.dot(hot, p_hi, preferred_element_type=F32)
                + jnp.dot(hot, p_lo, preferred_element_type=F32)
            )

        total = jnp.zeros((2 * mc, nr), F32)
        for g in range(na // span):
            total = gather_in(g, total)
        return total

    def part_out(o):
        return remote(
            part_snd.at[o], part_rcv.at[o], psend.at[0, o], precv.at[0, o], (ax, pitch_peer(o))
        )

    for o in range(1, npi):
        got_rows(o)
        part_snd[o] = injected(pitch_peer(o))
        part_out(o).start()
    got_rows(0)
    mine = injected(pz)
    for o in range(1, npi):
        part_out(o).wait_recv()
        mine = mine + part_rcv[o]
    inj[...] = mine

    row_e = lax.broadcasted_iota(jnp.int32, (8, nr), 0)

    @pl.loop(0, mc, unroll=4)
    def _(c):
        low = jnp.where(row_e == 0, inj[pl.ds(2 * c, 1), :], 0.0)
        high = jnp.where(row_e == 7, inj[pl.ds(2 * c + 1, 1), :], 0.0)
        res[c, 0:8, :] = res[c, 0:8, :] + low
        res[c, mt - 8:mt, :] = res[c, mt - 8:mt, :] + high
        da[c + 1, 0:8, :] = da[c + 1, 0:8, :] + low * (1.0 / THETA)
        da[c + 1, mt - 8:mt, :] = da[c + 1, mt - 8:mt, :] + high * (1.0 / THETA)

    mpack[1] = pack(da)
    start(mcopy[1])

    factors = cheb_factors()
    for sweep, (old, new) in enumerate(((da, db), (db, da))):
        st = sweep + 1
        comb = spans(st)
        ends(old, st)
        if sweep == 1:
            wait_sent(mcopy[1])
        f0, f1 = factors[sweep]

        def step(c, acc, old=old, new=new, comb=comb, f0=f0, f1=f1, sweep=sweep):
            tile, around = beside(old, comb, c)
            base = xpad[c + 1] if sweep == 0 else metal_out[c]
            metal_out[c] = base + tile
            left = res[c] - ((6.0 + diag[c]) * tile - around)
            res[c] = left
            fresh = f0 * tile + f1 * left
            new[c + 1] = fresh
            return pack_in(acc, fresh, c)

        mpack[st + 1] = lax.fori_loop(0, mc, step, jnp.zeros((mt, nr), F32), unroll=4)
        start(mcopy[st + 1])

    comb = spans(3)
    ends(da, 3)
    f0, f1 = factors[2]

    @pl.loop(0, mc, unroll=4)
    def _(c):
        tile, around = beside(da, comb, c)
        left = res[c] - ((6.0 + diag[c]) * tile - around)
        done = metal_out[c] + tile + (f0 * tile + f1 * left)
        metal_out[c] = done
        inj[pl.ds(2 * c, 1), :] = done[0:1]
        inj[pl.ds(2 * c + 1, 1), :] = done[mt - 1:mt]

    bound[0] = inj[...]

    def bound_out(o):
        return remote(
            bound.at[0], bound.at[o], psend.at[1, o], precv.at[1, o], (ax, pitch_peer(o))
        )

    for o in range(1, npi):
        bound_out(o).start()

    def block(ref, e):
        return ref.at[pl.ds(pl.multiple_of(e * cap, cap), cap)]

    def back_out(o, zo):
        i, z = axial_peer(o), lax.rem(pz - zo + npi, npi)
        return remote(
            block(bsnd, i * npi + z), block(brcv, ax * npi + z), asend.at[1, zo, o], arecv.at[1, zo, o],
            (i, pz),
        )

    def back_in(o, zo):
        i, z = lax.rem(ax - o + na, na), lax.rem(pz - zo + npi, npi)
        return remote(
            block(bsnd, i * npi + z), block(brcv, i * npi + z), asend.at[1, zo, o], arecv.at[1, zo, o],
            (i, pz),
        )

    for zo in range(npi):
        z = lax.rem(pz - zo + npi, npi)
        if zo:
            bound_out(zo).wait_recv()
        b_hi, b_lo = two_parts(bound[zo])
        bcat = jnp.concatenate([b_hi, b_lo], axis=1)
        for g in range(na // span):
            hot = place(g, z).T.astype(BF16)
            sums = jnp.dot(hot, bcat, preferred_element_type=F32)
            sums = sums[:, 0:nr] + sums[:, nr:2 * nr]
            for j in range(span):
                at = pl.multiple_of(((g * span + j) * npi + z) * cap, cap)
                bsnd[pl.ds(at, cap), :] = sums[j * cap:(j + 1) * cap]

        @pl.loop(1, na)
        def _(o, zo=zo):
            back_out(o, zo).start()

    own = pl.ds(pl.multiple_of(ax * npi * cap, npi * cap), npi * cap)
    brcv[own, :] = bsnd[own, :]

    wait_sent(first)
    wait_sent(second)
    wait_sent(mcopy[0])
    wait_sent(mcopy[2])
    wait_sent(mcopy[3])
    for zo in range(npi):

        @pl.loop(1, na)
        def _(o, zo=zo):
            out_copy(o, zo).wait_send()

    for o in range(1, npi):
        part_out(o).wait_send()
        bound_out(o).wait_send()
    for zo in range(npi):

        @pl.loop(1, na)
        def _(o, zo=zo):
            back_in(o, zo).wait_recv()

    @pl.loop(0, slots // 16)
    def _(i):
        for j in range(16):
            s = i * 16 + j
            rows[pl.ds(s, 1), :] = brcv[pl.ds(key_s[s], 1), :]

    live = lax.broadcasted_iota(jnp.int32, (slots, nr), 0) < count_s[0]
    wall_out[...] = jnp.where(live, 0.5 * (wall[...] + rows[...]), wall[...])

    for zo in range(npi):

        @pl.loop(1, na)
        def _(o, zo=zo):
            back_out(o, zo).wait_send()


def on_device(
    na, npi,
    fluid_temp, axial_speed, pitch_speed, fourier_store, wall_temp, wall_cell,
    wall_owner, wall_target, wall_count, metal_temp, metal_diag,
):
    devices = na * npi
    slots = wall_temp.shape[0]
    ca, cp, nr = fluid_temp.shape
    mc, mt, _ = metal_temp.shape
    cap = max(2, 2 * slots // devices)
    order = jnp.arange(slots, dtype=jnp.int32)
    live = order < wall_count[0]
    owner = wall_owner[:, 0]
    earlier = (owner[:, None] == owner[None, :]) & live[None, :] & (order[None, :] < order[:, None])
    rank = jnp.sum(earlier.astype(jnp.int32), axis=1)
    key = jnp.where(live, owner * cap + rank, -1)
    spots = jnp.arange(devices * cap, dtype=jnp.int32)
    ids = jnp.sum(
        jnp.where(spots[:, None] == key[None, :], (wall_target + 1).astype(F32)[None, :], 0.0), axis=1
    ).reshape(devices, 1, 1, cap)
    ids = jnp.broadcast_to(ids, (devices, 8, nr // cap, cap)).reshape(devices, 8, nr)
    cell_row = jnp.where(live, wall_cell, -1)[None, :]
    vmem = pl.BlockSpec(memory_space=pltpu.VMEM)
    smem = pl.BlockSpec(memory_space=pltpu.SMEM)
    hbm = pl.BlockSpec(memory_space=pl.ANY)
    dma = pltpu.SemaphoreType.DMA
    return pl.pallas_call(
        functools.partial(kernel, na, npi, cap),
        out_shape=(
            jax.ShapeDtypeStruct((ca, cp, nr), F32),
            jax.ShapeDtypeStruct((mc, mt, nr), F32),
            jax.ShapeDtypeStruct((slots, nr), F32),
        ),
        in_specs=[smem] * 3 + [vmem] * 8 + [hbm] * 2,
        out_specs=(vmem, vmem, vmem),
        scratch_shapes=[
            pltpu.VMEM((ca + 2, cp, nr), F32),
            pltpu.VMEM((ca + 2, cp, nr), F32),
            pltpu.VMEM((ca * cp, nr), F32),
            pltpu.VMEM((ca * cp, nr), F32),
            pltpu.VMEM((ca * cp, nr), F32),
            pltpu.VMEM((2, 2, ca, nr), F32),
            pltpu.VMEM((2, 2, ca, nr), F32),
            pltpu.VMEM((slots, 3 * nr), BF16),
            pltpu.VMEM((slots, nr), F32),
            pltpu.VMEM((slots, 2 * nr), BF16),
            pltpu.VMEM((mc + 2, mt, nr), F32),
            pltpu.VMEM((mc + 2, mt, nr), F32),
            pltpu.VMEM((mc + 2, mt, nr), F32),
            pltpu.VMEM((mc, mt, nr), F32),
            pltpu.VMEM((4, 4, mt, nr), F32),
            pltpu.VMEM((4, mt, nr), F32),
            pltpu.VMEM((2 * mc, nr), F32),
            pltpu.VMEM((devices, cap + 8, nr), F32),
            pltpu.VMEM((devices, cap + 8, nr), F32),
            pltpu.VMEM((devices * cap, nr), F32),
            pltpu.VMEM((devices * cap, nr), F32),
            pltpu.VMEM((npi, 2 * mc, nr), F32),
            pltpu.VMEM((npi, 2 * mc, nr), F32),
            pltpu.VMEM((npi, 2 * mc, nr), F32),
            dma((2,)),
            dma((2, 4)),
            dma((2, 4)),
            dma((4, 4)),
            dma((4, 4)),
            dma((2, npi, na)),
            dma((2, npi, na)),
            dma((2, npi)),
            dma((2, npi)),
        ],
        compiler_params=pltpu.CompilerParams(
            collective_id=0, has_side_effects=True, vmem_limit_bytes=56 * 1024 * 1024
        ),
        name="window",
    )(
        wall_cell, jnp.maximum(key, 0), wall_count,
        cell_row, key[None, :], ids, wall_temp, fourier_store, axial_speed, pitch_speed,
        metal_diag, fluid_temp, metal_temp,
    )


def solution(mesh):
    placed = (
        P("axial", "pitch", None),
        P("axial", "pitch", None),
        P("axial", "pitch", None),
        P(None, "axial", None),
        P(("axial", "pitch"), None),
        P(("axial", "pitch")),
        P(("axial", "pitch"), None),
        P(("axial", "pitch")),
        P(("axial", "pitch")),
        P("axial", None, "pitch"),
        P("axial", None, "pitch"),
    )
    return jax.shard_map(
        functools.partial(on_device, mesh.shape["axial"], mesh.shape["pitch"]),
        mesh=mesh,
        in_specs=placed,
        out_specs=(
            P("axial", "pitch", None),
            P("axial", None, "pitch"),
            P(("axial", "pitch"), None),
        ),
        check_vma=False,
    )
```
